32 devices in a mesh: dp: 4 (over z), mp: 8 (over y, x, core).
Axes of the slice: x: 2, y: 2, z: 4, core: 2. Of those that a mesh axis runs over, the one named last changes fastest.
Arguments:
- old_weight: float32 [768, 43008], P('dp', 'mp'), may hold values from -6 to 6
- old_first: float32 [768, 43008], P('dp', 'mp'), may hold values from -6 to 6
- old_second: float32 [768, 43008], P('dp', 'mp'), may hold values from 0.1 to 2
- gradient: float32 [768, 43008], P('dp', 'mp'), may hold values from -6 to 6
- old_rows: int32 [4, 192], replicated, may hold values from 0 to 767, as said below
- new_rows: int32 [4, 192], replicated, may hold values from 0 to 767, as said below
- new_units: int32 [8, 42], replicated, may hold values from 0 to 335, as said below
- step: int32 [1], replicated, may hold values from 1 to 49
Outputs:
- new_weight: float32 [768, 43008], P('dp', 'mp')
- new_first: float32 [768, 43008], P('dp', 'mp')
- new_second: float32 [768, 43008], P('dp', 'mp')
- update: float32 [768, 43008], P('dp', 'mp')
The draws below stay inside these ranges and needn't reach their ends.
Inputs may be any that keep to these rules, and one draw needn't show every extreme that they name: old_rows names every slab row once. Of the rows in one old data shard, at most 72 are named by any one new data shard, and in every draw each old data shard has exactly 72 for some new data shard. new_rows names every slab row once; the bound on rows from one old data shard to one new data shard, stated for old_rows, holds. new_units names every column unit once. Of the units u * 42 to u * 42 + 41 of old tensor shard u, at most 8 are named by any one new tensor shard, and in every draw each old tensor shard has exactly 8 for some new tensor shard.
All inputs are finite; a program needn't handle non-finite values.
Results may differ from the reference program's by a relative error of at most 0.00018.
Values sent between devices are 32-bit elements; how exact they have to be, the bound alone decides.
A program may use at most 128 MiB of HBM per device.

```python
import math
import jax
import jax.numpy as jnp

HEAD_DIM = 128
ROWS_DEV = 192
SLAB = 768
COLS = 43008
UNITS = 336
UNIT_DEV = 42


def shift_weights(key, shards, per_shard):
    base = per_shard // shards
    remain = per_shard % shards
    extra = base // 2
    index_set = jnp.arange(shards, dtype=jnp.int32)
    weights = base + (index_set < remain).astype(jnp.int32)
    weights = weights.at[0].add(extra).at[shards - 1].add(-extra)
    key_move, key_order = jax.random.split(key)
    moved = jax.random.randint(key_move, (), 0, max(extra, 1), dtype=jnp.int32)
    weights = weights.at[1].add(moved).at[shards - 2].add(-moved)
    return weights[jax.random.permutation(key_order, shards)].astype(jnp.int32)


def move_lists(key, shards, per_shard, old_flat):
    keys = jax.random.split(key, 4)
    weights = shift_weights(keys[0], shards, per_shard)
    sigma = jax.random.permutation(keys[1], shards).astype(jnp.int32)
    sigma_inv = jnp.argsort(sigma).astype(jnp.int32)
    source = jnp.arange(shards, dtype=jnp.int32)[:, None]
    target = jnp.arange(shards, dtype=jnp.int32)[None, :]
    counts = weights[(sigma_inv[target] - source) % shards]
    offsets = jnp.cumsum(counts, axis=0) - counts
    orders = jax.vmap(lambda sub: jax.random.permutation(sub, per_shard))(jax.random.split(keys[2], shards)).astype(jnp.int32)
    shuffles = jax.vmap(lambda sub: jax.random.permutation(sub, per_shard))(jax.random.split(keys[3], shards)).astype(jnp.int32)
    cumul = jnp.cumsum(weights).astype(jnp.int32)
    walker = jnp.arange(per_shard, dtype=jnp.int32)
    segment = jnp.searchsorted(cumul, walker, side='right').astype(jnp.int32)
    within = walker - (cumul - weights)[segment]
    dest = sigma[(source + segment[None, :]) % shards]
    arrive = offsets[source, dest] + within[None, :]
    new_slot = shuffles[dest, arrive]
    values = old_flat.reshape(shards, per_shard)[source, orders]
    spots = (dest * per_shard + new_slot).reshape(-1)
    new_flat = jnp.zeros((shards * per_shard,), jnp.int32).at[spots].set(values.reshape(-1).astype(jnp.int32))
    return new_flat.reshape(shards, per_shard)


def row_lists(key):
    shards = SLAB // ROWS_DEV
    old_flat = jax.random.permutation(jax.random.fold_in(key, 11), SLAB).astype(jnp.int32)
    new_list = move_lists(jax.random.fold_in(key, 12), shards, ROWS_DEV, old_flat)
    return (old_flat.reshape(shards, ROWS_DEV), new_list)


def draw_old_rows(key, part):
    both_lists = row_lists(key)
    return both_lists[0]


def draw_new_rows(key, part):
    both_lists = row_lists(key)
    return both_lists[1]


def draw_new_units(key, part):
    key = jax.random.fold_in(key, 3)
    shards = UNITS // UNIT_DEV
    old_flat = jnp.arange(UNITS, dtype=jnp.int32)
    return move_lists(key, shards, UNIT_DEV, old_flat)


def block_scale(stream_key, extent, cuts, least, largest):
    loudness = 1.0
    for axis_at, shards_of in cuts:
        heights = jax.random.uniform(jax.random.fold_in(jax.random.fold_in(stream_key, 6), axis_at), (shards_of,), jnp.float32, least / len(cuts), largest / len(cuts))
        loudness = loudness * jnp.repeat(jnp.exp(heights), extent[axis_at] // shards_of).reshape((-1,) + (1,) * (len(extent) - 1 - axis_at))
    return loudness


def gaussian(key, dims, scale, reach, cuts=(), kind=jnp.bfloat16):
    result = jax.random.normal(key, dims, jnp.float32) * scale
    if len(cuts) > 0:
        result = block_scale(key, dims, cuts, -0.22, 0.18) * result
    return jnp.clip(result, min=-reach, max=reach).astype(kind)


def setup_inputs(seed: int = 0) -> dict:
    key_list = jax.random.split(jax.random.key(seed), 9)
    old_weight = gaussian(key_list[0], (SLAB, COLS), 1.0, 6.0, ((0, 4), (1, 8)), jnp.float32)
    old_first = gaussian(key_list[1], (SLAB, COLS), 1.0, 6.0, ((0, 4), (1, 8)), jnp.float32)
    old_second = jnp.clip(jnp.exp(math.log(2.0) - 2.9957323 * jax.random.uniform(key_list[2], (SLAB, COLS), jnp.float32) ** block_scale(key_list[2], (SLAB, COLS), ((0, 4), (1, 8)), -0.2, 0.2)), 0.1, 2.0)
    gradient = gaussian(key_list[3], (SLAB, COLS), 1.0, 6.0, ((0, 4), (1, 8)), jnp.float32)
    old_rows = draw_old_rows(jax.random.fold_in(key_list[8], 71), 0)
    new_rows = draw_new_rows(jax.random.fold_in(key_list[8], 71), 0)
    new_units = draw_new_units(jax.random.fold_in(key_list[8], 71), 0)
    step = jax.random.randint(key_list[7], (1,), 1, 50).astype(jnp.int32)
    return {"old_weight": old_weight, "old_first": old_first, "old_second": old_second, "gradient": gradient, "old_rows": old_rows, "new_rows": new_rows, "new_units": new_units, "step": step}


beta_one = 0.9
beta_two = 0.999
epsilon = 1e-08
learn_rate = 0.001
decay_rate = 0.1

def adam_step(weight, first, second, gradient, step):
    step_count = step[0].astype(jnp.float32)
    new_first = beta_one * first + (1.0 - beta_one) * gradient
    new_second = beta_two * second + (1.0 - beta_two) * gradient * gradient
    first_fix = 1.0 - jnp.power(jnp.float32(beta_one), step_count)
    second_fix = 1.0 - jnp.power(jnp.float32(beta_two), step_count)
    update = new_first / first_fix / (jnp.sqrt(new_second / second_fix) + epsilon) + decay_rate * weight
    new_weight = weight - learn_rate * update
    return (new_weight, new_first, new_second, update)

def reference(old_weight, old_first, old_second, gradient, old_rows, new_rows, new_units, step):
    old_flat = old_rows.reshape(-1).astype(jnp.int32)
    new_flat = new_rows.reshape(-1).astype(jnp.int32)
    places = jnp.arange(SLAB, dtype=jnp.int32)
    old_place = jnp.zeros((SLAB,), jnp.int32).at[old_flat].set(places)
    picked = old_place[new_flat]
    unit_order = new_units.reshape(-1).astype(jnp.int32)

    def regroup(values):
        values = values[picked]
        values = values.reshape(SLAB, UNITS, HEAD_DIM)[:, unit_order, :]
        return values.reshape(SLAB, UNITS * HEAD_DIM)
    weight = regroup(old_weight)
    first = regroup(old_first)
    second = regroup(old_second)
    return adam_step(weight, first, second, gradient, step)
```

```python
import functools
import jax
import jax.numpy as jnp
from jax import lax
from jax.experimental import pallas as pl
from jax.experimental.pallas import tpu as pltpu
from jax.sharding import PartitionSpec as P

UNIT = 128
MESH = pl.DeviceIdType.MESH

beta_one = 0.9
beta_two = 0.999
epsilon = 1e-08
learn_rate = 0.001
decay_rate = 0.1


def room_for(count, shards):
    share = count // shards
    return share + share // 2 + min(count % shards, 1)


def iota(n):
    return jnp.arange(n, dtype=jnp.int32)


def row_plan(old_rows, new_rows, dp_index, room):
    shards, per = old_rows.shape
    old_flat = old_rows.reshape(-1)
    new_flat = new_rows.reshape(-1)
    total = shards * per
    same = (old_flat[:, None] == new_flat[None, :]).astype(jnp.int32)
    target = jnp.sum(same * (iota(total) // per)[None, :], axis=1).reshape(shards, per)
    earlier = (iota(per)[:, None] > iota(per)[None, :])[None]
    rank = jnp.sum(((target[:, :, None] == target[:, None, :]) & earlier).astype(jnp.int32), axis=2)
    my_target = lax.dynamic_index_in_dim(target, dp_index, 0, False)
    my_rank = lax.dynamic_index_in_dim(rank, dp_index, 0, False)
    shift = lax.rem(my_target - dp_index + shards, shards)
    spot = shift * room + my_rank
    pack = (iota(shards * room)[:, None] == spot[None, :]).astype(jnp.bfloat16)
    wanted = lax.dynamic_index_in_dim(new_rows, dp_index, 0, False)
    anchor = (iota(total) // per) * room + rank.reshape(-1)
    found = (wanted[:, None] == old_flat[None, :]).astype(jnp.int32)
    column = jnp.sum(found * anchor[None, :], axis=1)
    take = (column[:, None] == iota(shards * room)[None, :]).astype(jnp.bfloat16)
    return pack, take


def unit_plan(new_units, mp_index, chunks):
    shards, per = new_units.shape
    total = shards * per
    unit_flat = new_units.reshape(-1)
    same = (iota(total)[:, None] == unit_flat[None, :]).astype(jnp.int32)
    target = jnp.sum(same * (iota(total) // per)[None, :], axis=1).reshape(shards, per)
    ahead = (target[:, None, :] < target[:, :, None]) | (
        (target[:, None, :] == target[:, :, None])
        & (iota(per)[None, None, :] < iota(per)[None, :, None])
    )
    place = jnp.sum(ahead.astype(jnp.int32), axis=2)
    my_place = lax.dynamic_index_in_dim(place, mp_index, 0, False)
    my_target = lax.dynamic_index_in_dim(target, mp_index, 0, False)
    deep = -(-per // chunks)
    at = (iota(deep)[None, :] * chunks + iota(chunks)[:, None]).reshape(-1)
    order = jnp.sum((at[:, None] == my_place[None, :]).astype(jnp.int32) * iota(per)[None, :], axis=1)
    lane = my_place % chunks * shards + my_target
    slots = iota(chunks * shards)
    chosen = jnp.sum(
        (slots[:, None] == lane[None, :]).astype(jnp.int32) * (my_place // chunks)[None, :], axis=1
    )
    wanted = lax.dynamic_index_in_dim(new_units, mp_index, 0, False)
    arrive = (place % chunks * shards + iota(shards)[:, None]).reshape(-1)
    found = (wanted[:, None] == iota(total)[None, :]).astype(jnp.int32)
    landed = jnp.sum(found * arrive[None, :], axis=1)
    return order, chosen, landed


def exact_dot(onehot, values):
    width = values.shape[1]
    high = values.astype(jnp.bfloat16)
    rest = values - high.astype(jnp.float32)
    middle = rest.astype(jnp.bfloat16)
    low = (rest - middle.astype(jnp.float32)).astype(jnp.bfloat16)
    parts = jnp.concatenate([high, middle, low], axis=1)
    out = jnp.dot(onehot, parts, preferred_element_type=jnp.float32)
    return (out[:, :width] + out[:, width : 2 * width]) + out[:, 2 * width :]


def move_kernel(dp, mp, rows, units, room, chunks, *refs):
    order_ref, chosen_ref, pack_ref, take_ref = refs[:4]
    states = refs[4:7]
    out_ref = refs[7]
    scratch = refs[8:]
    arrive = scratch[:chunks]
    (held, leave, unit_leave, load_sem, row_send, row_recv, unit_send, unit_recv, own_sem) = scratch[
        chunks:
    ]
    me_dp = lax.axis_index("dp")
    me_mp = lax.axis_index("mp")
    deep = -(-units // chunks)

    def load(u, carry):
        for a in range(3):
            pltpu.make_async_copy(
                states[a].at[:, pl.ds(pl.multiple_of(u * UNIT, UNIT), UNIT)],
                held.at[a, u],
                load_sem.at[a],
            ).start()
        return carry

    lax.fori_loop(0, units, load, 0)
    barrier = pltpu.get_barrier_semaphore()
    for k in range(1, dp):
        pl.semaphore_signal(
            barrier, inc=1, device_id=(lax.rem(me_dp + k, dp), me_mp), device_id_type=MESH
        )
    for k in range(1, mp):
        pl.semaphore_signal(
            barrier, inc=1, device_id=(me_dp, lax.rem(me_mp + k, mp)), device_id_type=MESH
        )
    pl.semaphore_wait(barrier, dp + mp - 2)

    def count(j):
        return -(-(units - j) // chunks)

    def row_copy(j, k):
        n = count(j)
        return pltpu.make_async_remote_copy(
            src_ref=leave.at[j % 2, k - 1, pl.ds(0, n)],
            dst_ref=arrive[j].at[pl.ds(0, n), :, pl.ds(pl.multiple_of(me_dp * room, 8), room), :],
            send_sem=row_send.at[j % 2, k - 1],
            recv_sem=row_recv.at[j, k - 1],
            device_id=(lax.rem(me_dp + k, dp), me_mp),
            device_id_type=MESH,
        )

    def pack(j):
        def one(w, carry):
            u = order_ref[j * deep + w]
            values = jnp.concatenate([held[a, u] for a in range(3)], axis=1)
            packed = exact_dot(pack_ref[...], values)
            for a in range(3):
                piece = packed[:, a * UNIT : (a + 1) * UNIT]
                arrive[j][w, a, pl.ds(pl.multiple_of(me_dp * room, 8), room), :] = piece[:room]
                for k in range(1, dp):
                    leave[j % 2, k - 1, w, a] = piece[k * room : (k + 1) * room]
            return carry

        lax.fori_loop(0, count(j), one, 0)
        for k in range(1, dp):
            row_copy(j, k).start()

    def unit_copy(j, k):
        peer = lax.rem(me_mp + k, mp)
        return pltpu.make_async_remote_copy(
            src_ref=unit_leave.at[j % 2, k],
            dst_ref=out_ref.at[j * mp + me_mp],
            send_sem=unit_send.at[j % 2, k],
            recv_sem=unit_recv.at[j, k],
            device_id=(me_dp, peer),
            device_id_type=MESH,
        )

    def own_copy(j):
        return pltpu.make_async_copy(
            unit_leave.at[j % 2, 0], out_ref.at[j * mp + me_mp], own_sem.at[j % 2]
        )

    def unpack(j):
        def one(k, carry):
            peer = lax.rem(me_mp + k, mp)
            w = chosen_ref[j * mp + peer]
            values = jnp.concatenate([arrive[j][w, a] for a in range(3)], axis=1)
            placed = exact_dot(take_ref[...], values)
            for a in range(3):
                unit_leave[j % 2, k, a] = placed[:, a * UNIT : (a + 1) * UNIT]
            return carry

        lax.fori_loop(0, mp, one, 0)
        for k in range(1, mp):
            unit_copy(j, k).start()
        own_copy(j).start()

    def wait_unit_send(j):
        for k in range(1, mp):
            unit_copy(j, k).wait_send()
        own_copy(j).wait()

    for a in range(3):
        pltpu.make_async_copy(held.at[a], held.at[a], load_sem.at[a]).wait()
    for j in range(min(2, chunks)):
        pack(j)
    for j in range(chunks):
        for k in range(1, dp):
            row_copy(j, k).wait_send()
        if j + 2 < chunks:
            pack(j + 2)
        for k in range(1, dp):
            row_copy(j, k).wait_recv()
        if j >= 2:
            wait_unit_send(j - 2)
        unpack(j)
    for j in range(max(chunks - 2, 0), chunks):
        wait_unit_send(j)
    for j in range(chunks):
        for k in range(1, mp):
            unit_copy(j, k).wait_recv()


def move(order, chosen, pack, take, states, dp, mp, rows, units, room, chunks):
    deep = -(-units // chunks)
    vmem = pl.BlockSpec(memory_space=pltpu.VMEM)
    smem = pl.BlockSpec(memory_space=pltpu.SMEM)
    f32 = jnp.float32
    return pl.pallas_call(
        functools.partial(move_kernel, dp, mp, rows, units, room, chunks),
        out_shape=jax.ShapeDtypeStruct((chunks * mp, 3, rows, UNIT), f32),
        in_specs=[smem, smem, vmem, vmem] + [pl.BlockSpec(memory_space=pl.ANY)] * 3,
        out_specs=pl.BlockSpec(memory_space=pl.ANY),
        scratch_shapes=[pltpu.VMEM((deep, 3, dp * room, UNIT), f32) for _ in range(chunks)]
        + [
            pltpu.VMEM((3, units, rows, UNIT), f32),
            pltpu.VMEM((2, dp - 1, deep, 3, room, UNIT), f32),
            pltpu.VMEM((2, mp, 3, rows, UNIT), f32),
            pltpu.SemaphoreType.DMA((3,)),
            pltpu.SemaphoreType.DMA((2, dp - 1)),
            pltpu.SemaphoreType.DMA((chunks, dp - 1)),
            pltpu.SemaphoreType.DMA((2, mp)),
            pltpu.SemaphoreType.DMA((chunks, mp)),
            pltpu.SemaphoreType.DMA((2,)),
        ],
        compiler_params=pltpu.CompilerParams(
            collective_id=0, has_side_effects=True, vmem_limit_bytes=60 * 2**20
        ),
    )(order, chosen, pack, take, *states)


def adam_kernel(group, landed_ref, fix_ref, *refs):
    moved = refs[:group]
    gradient_ref = refs[group]
    weight_out, first_out, second_out, update_out = refs[group + 1 :]
    first_fix = fix_ref[0]
    second_fix = fix_ref[1]
    for g in range(group):
        at = slice(g * UNIT, (g + 1) * UNIT)
        weight, first, second = moved[g][0, 0], moved[g][0, 1], moved[g][0, 2]
        gradient = gradient_ref[:, at]
        new_first = beta_one * first + (1.0 - beta_one) * gradient
        new_second = beta_two * second + (1.0 - beta_two) * gradient * gradient
        update = (
            new_first / first_fix / (jnp.sqrt(new_second / second_fix) + epsilon)
            + decay_rate * weight
        )
        weight_out[:, at] = weight - learn_rate * update
        first_out[:, at] = new_first
        second_out[:, at] = new_second
        update_out[:, at] = update


def adam(landed, fixes, moved, gradient):
    rows, columns = gradient.shape
    units = columns // UNIT
    group = next(g for g in (3, 2, 1) if units % g == 0)
    wide = pl.BlockSpec((rows, group * UNIT), lambda i, landed: (0, i))
    picks = [
        pl.BlockSpec((1, 3, rows, UNIT), lambda i, landed, g=g: (landed[i * group + g], 0, 0, 0))
        for g in range(group)
    ]
    return pl.pallas_call(
        functools.partial(adam_kernel, group),
        out_shape=[jax.ShapeDtypeStruct((rows, columns), jnp.float32)] * 4,
        grid_spec=pltpu.PrefetchScalarGridSpec(
            num_scalar_prefetch=1,
            grid=(units // group,),
            in_specs=[pl.BlockSpec(memory_space=pltpu.SMEM)] + picks + [wide],
            out_specs=[wide] * 4,
        ),
        compiler_params=pltpu.CompilerParams(vmem_limit_bytes=32 * 2**20),
    )(landed, fixes, *([moved] * group), gradient)


def body(old_weight, old_first, old_second, gradient, old_rows, new_rows, new_units, step):
    dp = lax.axis_size("dp")
    mp = lax.axis_size("mp")
    rows = old_weight.shape[0]
    units = new_units.shape[1]
    room = -(-room_for(rows, dp) // 8) * 8
    chunks = room_for(units, mp)
    pack, take = row_plan(old_rows, new_rows, lax.axis_index("dp"), room)
    order, chosen, landed = unit_plan(new_units, lax.axis_index("mp"), chunks)
    moved = move(
        order,
        chosen,
        pack,
        take,
        (old_weight, old_first, old_second),
        dp,
        mp,
        rows,
        units,
        room,
        chunks,
    )
    count = step[0].astype(jnp.float32)
    fixes = jnp.stack(
        [
            1.0 - jnp.power(jnp.float32(beta_one), count),
            1.0 - jnp.power(jnp.float32(beta_two), count),
        ]
    )
    return tuple(adam(landed, fixes, moved, gradient))


def solution(mesh):
    return jax.shard_map(
        body,
        mesh=mesh,
        in_specs=(P("dp", "mp"), P("dp", "mp"), P("dp", "mp"), P("dp", "mp"), P(), P(), P(), P()),
        out_specs=(P("dp", "mp"), P("dp", "mp"), P("dp", "mp"), P("dp", "mp")),
        check_vma=False,
    )
```

```python
import functools
import jax
import jax.numpy as jnp
from jax import lax
from jax.experimental import pallas as pl
from jax.experimental.pallas import tpu as pltpu
from jax.sharding import PartitionSpec as P

UNIT = 128
MESH = pl.DeviceIdType.MESH

beta_one = 0.9
beta_two = 0.999
epsilon = 1e-08
learn_rate = 0.001
decay_rate = 0.1


def room_for(count, shards):
    share = count // shards
    return share + share // 2 + min(count % shards, 1)


def iota(n):
    return jnp.arange(n, dtype=jnp.int32)


def row_targets(old_rows, new_rows):
    shards, per = old_rows.shape
    same = (old_rows.reshape(-1)[:, None] == new_rows.reshape(-1)[None, :]).astype(jnp.int32)
    return jnp.sum(same * (iota(shards * per) // per)[None, :], axis=1)


def row_needs(target, shards, per):
    source = iota(shards * per) // per
    cuts = iota(shards - 1)[:, None]
    right = (source[None, :] <= cuts) & (target[None, :] > cuts)
    left = (source[None, :] > cuts) & (target[None, :] <= cuts)
    counts = jnp.sum(jnp.stack([right, left]).astype(jnp.int32), axis=2)
    return jnp.max(counts)


def row_streams(target, old_rows, new_rows, me):
    shards, per = old_rows.shape
    total = shards * per
    source = iota(total) // per
    right_in = (source < me) & (target >= me)
    right_out = (source <= me) & (target > me)
    left_in = (source > me) & (target <= me)
    left_out = (source >= me) & (target < me)
    masks = jnp.stack([right_in, right_out, left_in, left_out])
    earlier = (iota(total)[:, None] < iota(total)[None, :]).astype(jnp.bfloat16)
    ranks = jnp.dot(
        masks.astype(jnp.bfloat16), earlier, preferred_element_type=jnp.float32
    ).astype(jnp.int32)
    place = jnp.where(masks, ranks, -1)
    local = jnp.where(source == me, iota(total) - me * per, -1)
    wanted = lax.dynamic_index_in_dim(new_rows, me, 0, False)
    found = (wanted[:, None] == old_rows.reshape(-1)[None, :]).astype(jnp.int32)
    taken = jnp.sum(
        found[None] * (jnp.stack([local, place[0], place[2]]) + 1)[:, None, :], axis=2
    ) - 1
    return local, place, taken


def row_matrices(local, place, taken, me, per, room):
    bf16 = jnp.bfloat16
    mine = lax.dynamic_slice_in_dim(place, me * per, per, axis=1)

    def by_own(out):
        return (iota(room)[:, None] == out[None, :]).astype(bf16)

    def by_stream(out, arriving):
        hit_out = (iota(room)[:, None] == out[None, :]).astype(bf16)
        hit_in = (arriving[:, None] == iota(room)[None, :]).astype(bf16)
        return jnp.dot(hit_out, hit_in, preferred_element_type=jnp.float32).astype(bf16)

    return (
        by_own(mine[1]),
        by_stream(place[1], place[0]),
        by_own(mine[3]),
        by_stream(place[3], place[2]),
        (taken[0][:, None] == iota(per)[None, :]).astype(bf16),
        (taken[1][:, None] == iota(room)[None, :]).astype(bf16),
        (taken[2][:, None] == iota(room)[None, :]).astype(bf16),
    )


def unit_plan(new_units, mp_index, chunks):
    shards, per = new_units.shape
    total = shards * per
    unit_flat = new_units.reshape(-1)
    same = (iota(total)[:, None] == unit_flat[None, :]).astype(jnp.int32)
    target = jnp.sum(same * (iota(total) // per)[None, :], axis=1).reshape(shards, per)
    ahead = (target[:, None, :] < target[:, :, None]) | (
        (target[:, None, :] == target[:, :, None])
        & (iota(per)[None, None, :] < iota(per)[None, :, None])
    )
    place = jnp.sum(ahead.astype(jnp.int32), axis=2)
    my_place = lax.dynamic_index_in_dim(place, mp_index, 0, False)
    my_target = lax.dynamic_index_in_dim(target, mp_index, 0, False)
    chunk = my_place % chunks
    begin = chunk * (per // chunks) + jnp.minimum(chunk, per % chunks)
    at = begin + my_place // chunks
    order = jnp.sum((iota(per)[:, None] == at[None, :]).astype(jnp.int32) * iota(per)[None, :], axis=1)
    lane = chunk * shards + my_target
    slots = iota(chunks * shards)
    chosen = jnp.sum(
        (slots[:, None] == lane[None, :]).astype(jnp.int32) * (my_place // chunks)[None, :], axis=1
    )
    wanted = lax.dynamic_index_in_dim(new_units, mp_index, 0, False)
    arrive = (place % chunks * shards + iota(shards)[:, None]).reshape(-1)
    found = (wanted[:, None] == iota(total)[None, :]).astype(jnp.int32)
    landed = jnp.sum(found * arrive[None, :], axis=1)
    return order, chosen, landed


def exact_parts(values):
    high = values.astype(jnp.bfloat16)
    rest = values - high.astype(jnp.float32)
    middle = rest.astype(jnp.bfloat16)
    low = (rest - middle.astype(jnp.float32)).astype(jnp.bfloat16)
    return jnp.concatenate([high, middle, low], axis=1)


def exact_pick(pairs):
    out = None
    for onehot, parts in pairs:
        term = jnp.dot(onehot, parts, preferred_element_type=jnp.float32)
        out = term if out is None else out + term
    width = out.shape[1] // 3
    return (out[:, :width] + out[:, width : 2 * width]) + out[:, 2 * width :]


SLOTS = 3
SKEW = 2


def move_kernel(dp, mp, rows, units, room, chunks, *refs):
    order_ref, chosen_ref = refs[:2]
    right_own, right_fwd, left_own, left_fwd, new_own, new_right, new_left = refs[2:9]
    states = refs[9:12]
    out_ref = refs[12]
    (held, from_left, from_right, to_right, to_left, placed, unit_leave) = refs[13:20]
    (load_sem, right_send, right_recv, left_send, left_recv, unit_send, unit_recv, own_sem) = refs[20:]
    me = lax.axis_index("dp")
    me_mp = lax.axis_index("mp")
    last = dp - 1

    def load(u, carry):
        for a in range(3):
            pltpu.make_async_copy(
                states[a].at[:, pl.ds(pl.multiple_of(u * UNIT, UNIT), UNIT)],
                held.at[a, u],
                load_sem.at[a],
            ).start()
        return carry

    lax.fori_loop(0, units, load, 0)
    barrier = pltpu.get_barrier_semaphore()

    for k in (1, last):
        pl.semaphore_signal(
            barrier, inc=1, device_id=(lax.rem(me + k, dp), me_mp), device_id_type=MESH
        )
    for k in range(1, mp):
        pl.semaphore_signal(
            barrier, inc=1, device_id=(me, lax.rem(me_mp + k, mp)), device_id_type=MESH
        )
    pl.semaphore_wait(barrier, mp + 1)

    def right_copy(i):
        return pltpu.make_async_remote_copy(
            src_ref=to_right.at[lax.rem(i, SLOTS)],
            dst_ref=from_left.at[i],
            send_sem=right_send.at[lax.rem(i, SLOTS)],
            recv_sem=right_recv.at[i],
            device_id=(me + 1, me_mp),
            device_id_type=MESH,
        )

    def left_copy(i):
        return pltpu.make_async_remote_copy(
            src_ref=to_left.at[lax.rem(i, SLOTS)],
            dst_ref=from_right.at[i],
            send_sem=left_send.at[lax.rem(i, SLOTS)],
            recv_sem=left_recv.at[i],
            device_id=(me - 1, me_mp),
            device_id_type=MESH,
        )

    def own_parts(i):
        u = order_ref[i]
        return exact_parts(jnp.concatenate([held[a, u] for a in range(3)], axis=1))

    def stream_parts(ref, i, there):
        values = jnp.concatenate([ref[i, a] for a in range(3)], axis=1)
        return exact_parts(jnp.where(there, values, 0.0))

    def send_step(i, sends, receives, copy, stage, arriving, own, forward):
        @pl.when(sends & (i >= 0) & (i < units))
        def _():
            @pl.when(receives)
            def _():
                copy(i).wait_recv()

            @pl.when(i >= SLOTS)
            def _():
                copy(i - SLOTS).wait_send()

            picked = exact_pick(
                [(own[...], own_parts(i)), (forward[...], stream_parts(arriving, i, receives))]
            )
            for a in range(3):
                stage[lax.rem(i, SLOTS), a] = picked[:, a * UNIT : (a + 1) * UNIT]
            copy(i).start()

    def sends(t):
        send_step(
            t - SKEW * me, me < last, me > 0, right_copy, to_right, from_left, right_own, right_fwd
        )
        send_step(
            t - SKEW * (last - me), me > 0, me < last, left_copy, to_left, from_right, left_own, left_fwd
        )

    def place(i, w):
        @pl.when(me == last)
        def _():
            right_copy(i).wait_recv()

        @pl.when(me == 0)
        def _():
            left_copy(i).wait_recv()

        picked = exact_pick(
            [
                (new_own[...], own_parts(i)),
                (new_right[...], stream_parts(from_left, i, me > 0)),
                (new_left[...], stream_parts(from_right, i, me < last)),
            ]
        )
        for a in range(3):
            placed[w, a] = picked[:, a * UNIT : (a + 1) * UNIT]

    def unit_copy(j, k):
        return pltpu.make_async_remote_copy(
            src_ref=unit_leave.at[j % 2, k],
            dst_ref=out_ref.at[j * mp + me_mp],
            send_sem=unit_send.at[j % 2, k],
            recv_sem=unit_recv.at[j, k],
            device_id=(me, lax.rem(me_mp + k, mp)),
            device_id_type=MESH,
        )

    def own_copy(j):
        return pltpu.make_async_copy(
            unit_leave.at[j % 2, 0], out_ref.at[j * mp + me_mp], own_sem.at[j % 2]
        )

    def emit(j):
        def one(k, carry):
            w = chosen_ref[j * mp + lax.rem(me_mp + k, mp)]
            unit_leave[j % 2, k] = placed[w]
            return carry

        lax.fori_loop(0, mp, one, 0)
        for k in range(1, mp):
            unit_copy(j, k).start()
        own_copy(j).start()

    def wait_unit_send(j):
        for k in range(1, mp):
            unit_copy(j, k).wait_send()
        own_copy(j).wait()

    for a in range(3):
        pltpu.make_async_copy(held.at[a], held.at[a], load_sem.at[a]).wait()

    lead = SKEW * last

    def first_steps(t, carry):
        sends(t)
        return carry

    lax.fori_loop(0, lead, first_steps, 0)
    begin = 0
    for j in range(chunks):
        count = -(-(units - j) // chunks)

        def steps(w, carry, begin=begin):
            sends(begin + w + lead)
            place(begin + w, w)
            return carry

        lax.fori_loop(0, count, steps, 0)
        begin += count
        if j >= 2:
            wait_unit_send(j - 2)
        emit(j)

    for i in range(max(units - SLOTS, 0), units):

        @pl.when(me < last)
        def _():
            right_copy(i).wait_send()

        @pl.when(me > 0)
        def _():
            left_copy(i).wait_send()

    for j in range(max(chunks - 2, 0), chunks):
        wait_unit_send(j)
    for j in range(chunks):
        for k in range(1, mp):
            unit_copy(j, k).wait_recv()


def move(order, chosen, matrices, states, dp, mp, rows, units, room, chunks, collective_id):
    deep = -(-units // chunks)
    vmem = pl.BlockSpec(memory_space=pltpu.VMEM)
    smem = pl.BlockSpec(memory_space=pltpu.SMEM)
    f32 = jnp.float32
    dma = pltpu.SemaphoreType.DMA
    return pl.pallas_call(
        functools.partial(move_kernel, dp, mp, rows, units, room, chunks),
        out_shape=jax.ShapeDtypeStruct((chunks * mp, 3, rows, UNIT), f32),
        in_specs=[smem, smem] + [vmem] * 7 + [pl.BlockSpec(memory_space=pl.ANY)] * 3,
        out_specs=pl.BlockSpec(memory_space=pl.ANY),
        scratch_shapes=[
            pltpu.VMEM((3, units, rows, UNIT), f32),
            pltpu.VMEM((units, 3, room, UNIT), f32),
            pltpu.VMEM((units, 3, room, UNIT), f32),
            pltpu.VMEM((SLOTS, 3, room, UNIT), f32),
            pltpu.VMEM((SLOTS, 3, room, UNIT), f32),
            pltpu.VMEM((deep, 3, rows, UNIT), f32),
            pltpu.VMEM((2, mp, 3, rows, UNIT), f32),
            dma((3,)),
            dma((SLOTS,)),
            dma((units,)),
            dma((SLOTS,)),
            dma((units,)),
            dma((2, mp)),
            dma((chunks, mp)),
            dma((2,)),
        ],
        compiler_params=pltpu.CompilerParams(
            collective_id=collective_id, has_side_effects=True, vmem_limit_bytes=60 * 2**20
        ),
    )(order, chosen, *matrices, *states)


def move_any(order, chosen, target, old_rows, new_rows, states, me, mp, units, chunks):
    dp, per = old_rows.shape
    room = room_for(per, dp)
    target = target.reshape(dp, per)
    earlier = (iota(per)[:, None] > iota(per)[None, :])[None]
    rank = jnp.sum(((target[:, :, None] == target[:, None, :]) & earlier).astype(jnp.int32), axis=2)
    spot = lax.dynamic_index_in_dim(target * room + rank, me, 0, False)
    hit = (iota(dp * room)[:, None] == spot[None, :]).astype(jnp.int32)
    pack = jnp.sum(hit * iota(per)[None, :], axis=1)
    anchor = (iota(dp * per) // per) * room + rank.reshape(-1)
    wanted = lax.dynamic_index_in_dim(new_rows, me, 0, False)
    found = (wanted[:, None] == old_rows.reshape(-1)[None, :]).astype(jnp.int32)
    take = jnp.sum(found * anchor[None, :], axis=1)
    begin = jnp.array(
        [j * (units // chunks) + min(j, units % chunks) for j in range(chunks)], jnp.int32
    )
    slots = jnp.take(order, jnp.repeat(begin, mp) + chosen)
    moved = []
    for state in states:
        packed = jnp.take(state, pack, axis=0)
        arrived = lax.all_to_all(packed, "dp", split_axis=0, concat_axis=0, tiled=True)
        rowed = jnp.take(arrived, take, axis=0).reshape(per, units, UNIT)
        leave = jnp.take(rowed, slots, axis=1).reshape(per, chunks, mp, UNIT)
        came = lax.all_to_all(leave, "mp", split_axis=2, concat_axis=2, tiled=True)
        moved.append(came.reshape(per, chunks * mp, UNIT).transpose(1, 0, 2))
    return jnp.stack(moved, axis=1)


def adam_kernel(group, landed_ref, fix_ref, *refs):
    moved = refs[:group]
    gradient_ref = refs[group]
    weight_out, first_out, second_out, update_out = refs[group + 1 :]
    first_fix = fix_ref[0]
    second_fix = fix_ref[1]
    for g in range(group):
        at = slice(g * UNIT, (g + 1) * UNIT)
        weight, first, second = moved[g][0, 0], moved[g][0, 1], moved[g][0, 2]
        gradient = gradient_ref[:, at]
        new_first = beta_one * first + (1.0 - beta_one) * gradient
        new_second = beta_two * second + (1.0 - beta_two) * gradient * gradient
        update = (
            new_first / first_fix / (jnp.sqrt(new_second / second_fix) + epsilon)
            + decay_rate * weight
        )
        weight_out[:, at] = weight - learn_rate * update
        first_out[:, at] = new_first
        second_out[:, at] = new_second
        update_out[:, at] = update


def adam(landed, fixes, moved, gradient):
    rows, columns = gradient.shape
    units = columns // UNIT
    group = next(g for g in (3, 2, 1) if units % g == 0)
    wide = pl.BlockSpec((rows, group * UNIT), lambda i, landed: (0, i))
    picks = [
        pl.BlockSpec((1, 3, rows, UNIT), lambda i, landed, g=g: (landed[i * group + g], 0, 0, 0))
        for g in range(group)
    ]
    return pl.pallas_call(
        functools.partial(adam_kernel, group),
        out_shape=[jax.ShapeDtypeStruct((rows, columns), jnp.float32)] * 4,
        grid_spec=pltpu.PrefetchScalarGridSpec(
            num_scalar_prefetch=1,
            grid=(units // group,),
            in_specs=[pl.BlockSpec(memory_space=pltpu.SMEM)] + picks + [wide],
            out_specs=[wide] * 4,
        ),
        compiler_params=pltpu.CompilerParams(vmem_limit_bytes=32 * 2**20),
    )(landed, fixes, *([moved] * group), gradient)


def body(old_weight, old_first, old_second, gradient, old_rows, new_rows, new_units, step):
    dp = lax.axis_size("dp")
    mp = lax.axis_size("mp")
    rows = old_weight.shape[0]
    units = new_units.shape[1]
    chunks = room_for(units, mp)
    me = lax.axis_index("dp")
    order, chosen, landed = unit_plan(new_units, lax.axis_index("mp"), chunks)
    target = row_targets(old_rows, new_rows)
    local, place, taken = row_streams(target, old_rows, new_rows, me)
    states = (old_weight, old_first, old_second)
    even = rows * dp // 4
    rooms = (even, -(-even * 5 // 32) * 8)

    def moved_in(room, collective_id):
        matrices = row_matrices(local, place, taken, me, rows, room)
        return move(
            order, chosen, matrices, states, dp, mp, rows, units, room, chunks, collective_id
        )

    def moved_any():
        return move_any(
            order, chosen, target, old_rows, new_rows, states, me, mp, units, chunks
        )

    need = row_needs(target, dp, rows)
    moved = lax.switch(
        (need > rooms[0]).astype(jnp.int32) + (need > rooms[1]).astype(jnp.int32),
        [lambda: moved_in(rooms[0], 0), lambda: moved_in(rooms[1], 1), moved_any],
    )
    count = step[0].astype(jnp.float32)
    fixes = jnp.stack(
        [
            1.0 - jnp.power(jnp.float32(beta_one), count),
            1.0 - jnp.power(jnp.float32(beta_two), count),
        ]
    )
    return tuple(adam(landed, fixes, moved, gradient))


def solution(mesh):
    return jax.shard_map(
        body,
        mesh=mesh,
        in_specs=(P("dp", "mp"), P("dp", "mp"), P("dp", "mp"), P("dp", "mp"), P(), P(), P(), P()),
        out_specs=(P("dp", "mp"), P("dp", "mp"), P("dp", "mp"), P("dp", "mp")),
        check_vma=False,
    )
```

```python
import functools
import jax
import jax.numpy as jnp
from jax import lax
from jax.experimental import pallas as pl
from jax.experimental.pallas import tpu as pltpu
from jax.sharding import PartitionSpec as P

UNIT = 128
MESH = pl.DeviceIdType.MESH

beta_one = 0.9
beta_two = 0.999
epsilon = 1e-08
learn_rate = 0.001
decay_rate = 0.1


def room_for(count, shards):
    share = count // shards
    return share + share // 2 + min(count % shards, 1)


def iota(n):
    return jnp.arange(n, dtype=jnp.int32)


def row_targets(old_rows, new_rows):
    shards, per = old_rows.shape
    same = (old_rows.reshape(-1)[:, None] == new_rows.reshape(-1)[None, :]).astype(jnp.int32)
    return jnp.sum(same * (iota(shards * per) // per)[None, :], axis=1)


def row_needs(target, shards, per):
    source = iota(shards * per) // per
    cuts = iota(shards - 1)[:, None]
    right = (source[None, :] <= cuts) & (target[None, :] > cuts)
    left = (source[None, :] > cuts) & (target[None, :] <= cuts)
    counts = jnp.sum(jnp.stack([right, left]).astype(jnp.int32), axis=2)
    return jnp.max(counts)


def row_streams(target, old_rows, new_rows, me):
    shards, per = old_rows.shape
    total = shards * per
    source = iota(total) // per
    right_in = (source < me) & (target >= me)
    right_out = (source <= me) & (target > me)
    left_in = (source > me) & (target <= me)
    left_out = (source >= me) & (target < me)
    masks = jnp.stack([right_in, right_out, left_in, left_out])
    earlier = (iota(total)[:, None] < iota(total)[None, :]).astype(jnp.bfloat16)
    ranks = jnp.dot(
        masks.astype(jnp.bfloat16), earlier, preferred_element_type=jnp.float32
    ).astype(jnp.int32)
    place = jnp.where(masks, ranks, -1)
    local = jnp.where(source == me, iota(total) - me * per, -1)
    wanted = lax.dynamic_index_in_dim(new_rows, me, 0, False)
    found = (wanted[:, None] == old_rows.reshape(-1)[None, :]).astype(jnp.int32)
    taken = jnp.sum(
        found[None] * (jnp.stack([local, place[0], place[2]]) + 1)[:, None, :], axis=2
    ) - 1
    return local, place, taken


def row_matrices(local, place, taken, me, per, room):
    bf16 = jnp.bfloat16
    mine = lax.dynamic_slice_in_dim(place, me * per, per, axis=1)

    def by_own(out):
        return (iota(room)[:, None] == out[None, :]).astype(bf16)

    def by_stream(out, arriving):
        hit_out = (iota(room)[:, None] == out[None, :]).astype(bf16)
        hit_in = (arriving[:, None] == iota(room)[None, :]).astype(bf16)
        return jnp.dot(hit_out, hit_in, preferred_element_type=jnp.float32).astype(bf16)

    return (
        by_own(mine[1]),
        by_stream(place[1], place[0]),
        by_own(mine[3]),
        by_stream(place[3], place[2]),
        (taken[0][:, None] == iota(per)[None, :]).astype(bf16),
        (taken[1][:, None] == iota(room)[None, :]).astype(bf16),
        (taken[2][:, None] == iota(room)[None, :]).astype(bf16),
    )


def unit_plan(new_units, mp_index, chunks):
    shards, per = new_units.shape
    total = shards * per
    unit_flat = new_units.reshape(-1)
    same = (iota(total)[:, None] == unit_flat[None, :]).astype(jnp.int32)
    target = jnp.sum(same * (iota(total) // per)[None, :], axis=1).reshape(shards, per)
    ahead = (target[:, None, :] < target[:, :, None]) | (
        (target[:, None, :] == target[:, :, None])
        & (iota(per)[None, None, :] < iota(per)[None, :, None])
    )
    place = jnp.sum(ahead.astype(jnp.int32), axis=2)
    my_place = lax.dynamic_index_in_dim(place, mp_index, 0, False)
    my_target = lax.dynamic_index_in_dim(target, mp_index, 0, False)
    chunk = my_place % chunks
    begin = chunk * (per // chunks) + jnp.minimum(chunk, per % chunks)
    at = begin + my_place // chunks
    deep = -(-per // chunks)
    order = jnp.sum((iota(per)[:, None] == at[None, :]).astype(jnp.int32) * iota(per)[None, :], axis=1)
    lane = chunk * shards + my_target
    slots = iota(chunks * shards)
    chosen = jnp.sum(
        (slots[:, None] == lane[None, :]).astype(jnp.int32) * (at % deep)[None, :], axis=1
    )
    wanted = lax.dynamic_index_in_dim(new_units, mp_index, 0, False)
    arrive = (place % chunks * shards + iota(shards)[:, None]).reshape(-1)
    found = (wanted[:, None] == iota(total)[None, :]).astype(jnp.int32)
    landed = jnp.sum(found * arrive[None, :], axis=1)
    return order, chosen, landed


def exact_parts(values):
    high = values.astype(jnp.bfloat16)
    rest = values - high.astype(jnp.float32)
    middle = rest.astype(jnp.bfloat16)
    low = (rest - middle.astype(jnp.float32)).astype(jnp.bfloat16)
    return jnp.concatenate([high, middle, low], axis=1)


def exact_pick(pairs):
    out = None
    for onehot, parts in pairs:
        term = jnp.dot(onehot, parts, preferred_element_type=jnp.float32)
        out = term if out is None else out + term
    width = out.shape[1] // 3
    return (out[:, :width] + out[:, width : 2 * width]) + out[:, 2 * width :]


SLOTS = 3
SKEW = 2


def move_kernel(dp, mp, rows, units, room, chunks, *refs):
    order_ref, chosen_ref = refs[:2]
    right_own, right_fwd, left_own, left_fwd, new_own, new_right, new_left = refs[2:9]
    states = refs[9:12]
    out_ref = refs[12]
    (held, from_left, from_right, to_right, to_left, placed, unit_leave) = refs[13:20]
    (load_sem, right_send, right_recv, left_send, left_recv, unit_send, unit_recv, own_sem, tail_send, tail_recv) = refs[
        20:
    ]
    me = lax.axis_index("dp")
    me_mp = lax.axis_index("mp")
    last = dp - 1
    deep = -(-units // chunks)

    def load(u, carry):
        for a in range(3):
            pltpu.make_async_copy(
                states[a].at[:, pl.ds(pl.multiple_of(u * UNIT, UNIT), UNIT)],
                held.at[a, u],
                load_sem.at[a],
            ).start()
        return carry

    lax.fori_loop(0, units, load, 0)
    barrier = pltpu.get_barrier_semaphore()

    for k in (1, last):
        pl.semaphore_signal(
            barrier, inc=1, device_id=(lax.rem(me + k, dp), me_mp), device_id_type=MESH
        )
    for k in range(1, mp):
        pl.semaphore_signal(
            barrier, inc=1, device_id=(me, lax.rem(me_mp + k, mp)), device_id_type=MESH
        )
    pl.semaphore_wait(barrier, mp + 1)

    def right_copy(i):
        return pltpu.make_async_remote_copy(
            src_ref=to_right.at[lax.rem(i, SLOTS)],
            dst_ref=from_left.at[i],
            send_sem=right_send.at[lax.rem(i, SLOTS)],
            recv_sem=right_recv.at[i],
            device_id=(me + 1, me_mp),
            device_id_type=MESH,
        )

    def left_copy(i):
        return pltpu.make_async_remote_copy(
            src_ref=to_left.at[lax.rem(i, SLOTS)],
            dst_ref=from_right.at[i],
            send_sem=left_send.at[lax.rem(i, SLOTS)],
            recv_sem=left_recv.at[i],
            device_id=(me - 1, me_mp),
            device_id_type=MESH,
        )

    starts = [j * (units // chunks) + min(j, units % chunks) for j in range(chunks + 1)]
    final = starts[chunks - 1]
    tail = units - final

    def piece(i, q):
        p = jnp.maximum(i - final, 0) * 3 + q
        early = i < final
        return jnp.where(early, q, p // tail), jnp.where(early, i, final + lax.rem(p, tail))

    def own_parts(i):
        pieces = []
        for q in range(3):
            a, at = piece(i, q)
            pieces.append(held[a, order_ref[at]])
        return exact_parts(jnp.concatenate(pieces, axis=1))

    def stream_parts(ref, i, there):
        values = jnp.concatenate([ref[i, a] for a in range(3)], axis=1)
        return exact_parts(jnp.where(there, values, 0.0))

    def send_step(i, sends, receives, copy, stage, arriving, own, forward):
        @pl.when(sends & (i >= 0) & (i < units))
        def _():
            @pl.when(receives)
            def _():
                copy(i).wait_recv()

            @pl.when(i >= SLOTS)
            def _():
                copy(i - SLOTS).wait_send()

            picked = exact_pick(
                [(own[...], own_parts(i)), (forward[...], stream_parts(arriving, i, receives))]
            )
            for a in range(3):
                stage[lax.rem(i, SLOTS), a] = picked[:, a * UNIT : (a + 1) * UNIT]
            copy(i).start()

    def sends(t):
        send_step(
            t - SKEW * me, me < last, me > 0, right_copy, to_right, from_left, right_own, right_fwd
        )
        send_step(
            t - SKEW * (last - me), me > 0, me < last, left_copy, to_left, from_right, left_own, left_fwd
        )

    def place(i):
        @pl.when(me == last)
        def _():
            right_copy(i).wait_recv()

        @pl.when(me == 0)
        def _():
            left_copy(i).wait_recv()

        picked = exact_pick(
            [
                (new_own[...], own_parts(i)),
                (new_right[...], stream_parts(from_left, i, me > 0)),
                (new_left[...], stream_parts(from_right, i, me < last)),
            ]
        )
        for q in range(3):
            a, at = piece(i, q)
            placed[lax.rem(at, deep), a] = picked[:, q * UNIT : (q + 1) * UNIT]

    def unit_copy(j, k):
        return pltpu.make_async_remote_copy(
            src_ref=unit_leave.at[j % 2, k],
            dst_ref=out_ref.at[j * mp + me_mp],
            send_sem=unit_send.at[j % 2, k],
            recv_sem=unit_recv.at[j, k],
            device_id=(me, lax.rem(me_mp + k, mp)),
            device_id_type=MESH,
        )

    def own_copy(j):
        return pltpu.make_async_copy(
            unit_leave.at[j % 2, 0], out_ref.at[j * mp + me_mp], own_sem.at[j % 2]
        )

    def tail_copy(a, k):
        j = chunks - 1
        return pltpu.make_async_remote_copy(
            src_ref=unit_leave.at[j % 2, k, a],
            dst_ref=out_ref.at[j * mp + me_mp, a],
            send_sem=tail_send.at[a, k],
            recv_sem=tail_recv.at[a, k],
            device_id=(me, lax.rem(me_mp + k, mp)),
            device_id_type=MESH,
        )

    def tail_own(a):
        j = chunks - 1
        return pltpu.make_async_copy(
            unit_leave.at[j % 2, 0, a], out_ref.at[j * mp + me_mp, a], tail_send.at[a, 0]
        )

    def gather(j, arrays):
        def one(k, carry):
            w = chosen_ref[j * mp + lax.rem(me_mp + k, mp)]
            for a in arrays:
                unit_leave[j % 2, k, a] = placed[w, a]
            return carry

        lax.fori_loop(0, mp, one, 0)

    def wait_unit_send(j):
        for k in range(1, mp):
            unit_copy(j, k).wait_send()
        own_copy(j).wait()

    def emit(j):
        if j >= 2:
            wait_unit_send(j - 2)
        gather(j, range(3))
        for k in range(1, mp):
            unit_copy(j, k).start()
        own_copy(j).start()

    def emit_tail(a):
        if a == 0 and chunks >= 3:
            wait_unit_send(chunks - 3)
        gather(chunks - 1, [a])
        for k in range(1, mp):
            tail_copy(a, k).start()
        tail_own(a).start()

    for a in range(3):
        pltpu.make_async_copy(held.at[a], held.at[a], load_sem.at[a]).wait()

    lead = SKEW * last

    def step(t, carry):
        sends(t)
        i = t - lead

        @pl.when(i >= 0)
        def _():
            place(i)

        for j in range(chunks - 1):

            @pl.when(i == starts[j + 1] - 1)
            def _():
                emit(j)

        for a in range(3):

            @pl.when(i == final - 1 + -(-tail * (a + 1) // 3))
            def _():
                emit_tail(a)

        return carry

    lax.fori_loop(0, lead + units, step, 0)

    for i in range(max(units - SLOTS, 0), units):

        @pl.when(me < last)
        def _():
            right_copy(i).wait_send()

        @pl.when(me > 0)
        def _():
            left_copy(i).wait_send()

    if chunks >= 2:
        wait_unit_send(chunks - 2)
    for a in range(3):
        for k in range(1, mp):
            tail_copy(a, k).wait_send()
        tail_own(a).wait()
    for j in range(chunks - 1):
        for k in range(1, mp):
            unit_copy(j, k).wait_recv()
    for a in range(3):
        for k in range(1, mp):
            tail_copy(a, k).wait_recv()


def move(order, chosen, matrices, states, dp, mp, rows, units, room, chunks, collective_id):
    deep = -(-units // chunks)
    vmem = pl.BlockSpec(memory_space=pltpu.VMEM)
    smem = pl.BlockSpec(memory_space=pltpu.SMEM)
    f32 = jnp.float32
    dma = pltpu.SemaphoreType.DMA
    return pl.pallas_call(
        functools.partial(move_kernel, dp, mp, rows, units, room, chunks),
        out_shape=jax.ShapeDtypeStruct((chunks * mp, 3, rows, UNIT), f32),
        in_specs=[smem, smem] + [vmem] * 7 + [pl.BlockSpec(memory_space=pl.ANY)] * 3,
        out_specs=pl.BlockSpec(memory_space=pl.ANY),
        scratch_shapes=[
            pltpu.VMEM((3, units, rows, UNIT), f32),
            pltpu.VMEM((units, 3, room, UNIT), f32),
            pltpu.VMEM((units, 3, room, UNIT), f32),
            pltpu.VMEM((SLOTS, 3, room, UNIT), f32),
            pltpu.VMEM((SLOTS, 3, room, UNIT), f32),
            pltpu.VMEM((deep, 3, rows, UNIT), f32),
            pltpu.VMEM((2, mp, 3, rows, UNIT), f32),
            dma((3,)),
            dma((SLOTS,)),
            dma((units,)),
            dma((SLOTS,)),
            dma((units,)),
            dma((2, mp)),
            dma((chunks, mp)),
            dma((2,)),
            dma((3, mp)),
            dma((3, mp)),
        ],
        compiler_params=pltpu.CompilerParams(
            collective_id=collective_id, has_side_effects=True, vmem_limit_bytes=60 * 2**20
        ),
    )(order, chosen, *matrices, *states)


def move_any(order, chosen, target, old_rows, new_rows, states, me, mp, units, chunks):
    dp, per = old_rows.shape
    room = room_for(per, dp)
    target = target.reshape(dp, per)
    earlier = (iota(per)[:, None] > iota(per)[None, :])[None]
    rank = jnp.sum(((target[:, :, None] == target[:, None, :]) & earlier).astype(jnp.int32), axis=2)
    spot = lax.dynamic_index_in_dim(target * room + rank, me, 0, False)
    hit = (iota(dp * room)[:, None] == spot[None, :]).astype(jnp.int32)
    pack = jnp.sum(hit * iota(per)[None, :], axis=1)
    anchor = (iota(dp * per) // per) * room + rank.reshape(-1)
    wanted = lax.dynamic_index_in_dim(new_rows, me, 0, False)
    found = (wanted[:, None] == old_rows.reshape(-1)[None, :]).astype(jnp.int32)
    take = jnp.sum(found * anchor[None, :], axis=1)
    begin = jnp.array(
        [j * (units // chunks) + min(j, units % chunks) for j in range(chunks)], jnp.int32
    )
    deep = -(-units // chunks)
    first = jnp.repeat(begin, mp)
    slots = jnp.take(order, first + (chosen - first + deep * chunks) % deep, mode="clip")
    moved = []
    for state in states:
        packed = jnp.take(state, pack, axis=0)
        arrived = lax.all_to_all(packed, "dp", split_axis=0, concat_axis=0, tiled=True)
        rowed = jnp.take(arrived, take, axis=0).reshape(per, units, UNIT)
        leave = jnp.take(rowed, slots, axis=1).reshape(per, chunks, mp, UNIT)
        came = lax.all_to_all(leave, "mp", split_axis=2, concat_axis=2, tiled=True)
        moved.append(came.reshape(per, chunks * mp, UNIT).transpose(1, 0, 2))
    return jnp.stack(moved, axis=1)


def adam_kernel(group, landed_ref, fix_ref, *refs):
    moved = refs[:group]
    gradient_ref = refs[group]
    weight_out, first_out, second_out, update_out = refs[group + 1 :]
    first_fix = fix_ref[0]
    second_fix = fix_ref[1]
    for g in range(group):
        at = slice(g * UNIT, (g + 1) * UNIT)
        weight, first, second = moved[g][0, 0], moved[g][0, 1], moved[g][0, 2]
        gradient = gradient_ref[:, at]
        new_first = beta_one * first + (1.0 - beta_one) * gradient
        new_second = beta_two * second + (1.0 - beta_two) * gradient * gradient
        update = (
            new_first / first_fix / (jnp.sqrt(new_second / second_fix) + epsilon)
            + decay_rate * weight
        )
        weight_out[:, at] = weight - learn_rate * update
        first_out[:, at] = new_first
        second_out[:, at] = new_second
        update_out[:, at] = update


def adam(landed, fixes, moved, gradient):
    rows, columns = gradient.shape
    units = columns // UNIT
    group = next(g for g in (3, 2, 1) if units % g == 0)
    wide = pl.BlockSpec((rows, group * UNIT), lambda i, landed: (0, i))
    picks = [
        pl.BlockSpec((1, 3, rows, UNIT), lambda i, landed, g=g: (landed[i * group + g], 0, 0, 0))
        for g in range(group)
    ]
    return pl.pallas_call(
        functools.partial(adam_kernel, group),
        out_shape=[jax.ShapeDtypeStruct((rows, columns), jnp.float32)] * 4,
        grid_spec=pltpu.PrefetchScalarGridSpec(
            num_scalar_prefetch=1,
            grid=(units // group,),
            in_specs=[pl.BlockSpec(memory_space=pltpu.SMEM)] + picks + [wide],
            out_specs=[wide] * 4,
        ),
        compiler_params=pltpu.CompilerParams(vmem_limit_bytes=32 * 2**20),
    )(landed, fixes, *([moved] * group), gradient)


def body(old_weight, old_first, old_second, gradient, old_rows, new_rows, new_units, step):
    dp = lax.axis_size("dp")
    mp = lax.axis_size("mp")
    rows = old_weight.shape[0]
    units = new_units.shape[1]
    chunks = room_for(units, mp)
    me = lax.axis_index("dp")
    order, chosen, landed = unit_plan(new_units, lax.axis_index("mp"), chunks)
    target = row_targets(old_rows, new_rows)
    local, place, taken = row_streams(target, old_rows, new_rows, me)
    states = (old_weight, old_first, old_second)
    even = rows * dp // 4
    rooms = (even, -(-even * 5 // 32) * 8)

    count = step[0].astype(jnp.float32)
    fixes = jnp.stack(
        [
            1.0 - jnp.power(jnp.float32(beta_one), count),
            1.0 - jnp.power(jnp.float32(beta_two), count),
        ]
    )

    def moved_in(room, collective_id):
        matrices = row_matrices(local, place, taken, me, rows, room)
        moved = move(
            order, chosen, matrices, states, dp, mp, rows, units, room, chunks, collective_id
        )
        return adam(landed, fixes, moved, gradient)

    def moved_any():
        moved = move_any(
            order, chosen, target, old_rows, new_rows, states, me, mp, units, chunks
        )
        return adam(landed, fixes, moved, gradient)

    need = row_needs(target, dp, rows)
    outs = lax.switch(
        (need > rooms[0]).astype(jnp.int32) + (need > rooms[1]).astype(jnp.int32),
        [lambda: moved_in(rooms[0], 0), lambda: moved_in(rooms[1], 1), moved_any],
    )
    return tuple(outs)


def solution(mesh):
    return jax.shard_map(
        body,
        mesh=mesh,
        in_specs=(P("dp", "mp"), P("dp", "mp"), P("dp", "mp"), P("dp", "mp"), P(), P(), P(), P()),
        out_specs=(P("dp", "mp"), P("dp", "mp"), P("dp", "mp"), P("dp", "mp")),
        check_vma=False,
    )
```

```python
import functools
import jax
import jax.numpy as jnp
from jax import lax
from jax.experimental import pallas as pl
from jax.experimental.pallas import tpu as pltpu
from jax.sharding import PartitionSpec as P

UNIT = 128
MESH = pl.DeviceIdType.MESH

beta_one = 0.9
beta_two = 0.999
epsilon = 1e-08
learn_rate = 0.001
decay_rate = 0.1


def room_for(count, shards):
    share = count // shards
    return share + share // 2 + min(count % shards, 1)


def iota(n):
    return jnp.arange(n, dtype=jnp.int32)


def row_targets(old_rows, new_rows):
    shards, per = old_rows.shape
    same = (old_rows.reshape(-1)[:, None] == new_rows.reshape(-1)[None, :]).astype(jnp.int32)
    return jnp.sum(same * (iota(shards * per) // per)[None, :], axis=1)


def row_needs(target, shards, per):
    source = iota(shards * per) // per
    cuts = iota(shards - 1)[:, None]
    right = (source[None, :] <= cuts) & (target[None, :] > cuts)
    left = (source[None, :] > cuts) & (target[None, :] <= cuts)
    counts = jnp.sum(jnp.stack([right, left]).astype(jnp.int32), axis=2)
    return jnp.max(counts)


def row_streams(target, old_rows, new_rows, me):
    shards, per = old_rows.shape
    total = shards * per
    source = iota(total) // per
    right_in = (source < me) & (target >= me)
    right_out = (source <= me) & (target > me)
    left_in = (source > me) & (target <= me)
    left_out = (source >= me) & (target < me)
    masks = jnp.stack([right_in, right_out, left_in, left_out])
    earlier = (iota(total)[:, None] < iota(total)[None, :]).astype(jnp.bfloat16)
    ranks = jnp.dot(
        masks.astype(jnp.bfloat16), earlier, preferred_element_type=jnp.float32
    ).astype(jnp.int32)
    place = jnp.where(masks, ranks, -1)
    local = jnp.where(source == me, iota(total) - me * per, -1)
    wanted = lax.dynamic_index_in_dim(new_rows, me, 0, False)
    found = (wanted[:, None] == old_rows.reshape(-1)[None, :]).astype(jnp.int32)
    taken = jnp.sum(
        found[None] * (jnp.stack([local, place[0], place[2]]) + 1)[:, None, :], axis=2
    ) - 1
    return local, place, taken


def row_matrices(local, place, taken, me, per, room):
    bf16 = jnp.bfloat16
    mine = lax.dynamic_slice_in_dim(place, me * per, per, axis=1)

    def by_own(out):
        return (iota(room)[:, None] == out[None, :]).astype(bf16)

    def by_stream(out, arriving):
        hit_out = (iota(room)[:, None] == out[None, :]).astype(bf16)
        hit_in = (arriving[:, None] == iota(room)[None, :]).astype(bf16)
        return jnp.dot(hit_out, hit_in, preferred_element_type=jnp.float32).astype(bf16)

    return (
        by_own(mine[1]),
        by_stream(place[1], place[0]),
        by_own(mine[3]),
        by_stream(place[3], place[2]),
        (taken[0][:, None] == iota(per)[None, :]).astype(bf16),
        (taken[1][:, None] == iota(room)[None, :]).astype(bf16),
        (taken[2][:, None] == iota(room)[None, :]).astype(bf16),
    )


def unit_plan(new_units, mp_index, chunks):
    shards, per = new_units.shape
    total = shards * per
    unit_flat = new_units.reshape(-1)
    same = (iota(total)[:, None] == unit_flat[None, :]).astype(jnp.int32)
    target = jnp.sum(same * (iota(total) // per)[None, :], axis=1).reshape(shards, per)
    ahead = (target[:, None, :] < target[:, :, None]) | (
        (target[:, None, :] == target[:, :, None])
        & (iota(per)[None, None, :] < iota(per)[None, :, None])
    )
    place = jnp.sum(ahead.astype(jnp.int32), axis=2)
    my_place = lax.dynamic_index_in_dim(place, mp_index, 0, False)
    my_target = lax.dynamic_index_in_dim(target, mp_index, 0, False)
    chunk = my_place % chunks
    begin = chunk * (per // chunks) + jnp.minimum(chunk, per % chunks)
    at = begin + my_place // chunks
    deep = -(-per // chunks)
    order = jnp.sum((iota(per)[:, None] == at[None, :]).astype(jnp.int32) * iota(per)[None, :], axis=1)
    lane = chunk * shards + my_target
    slots = iota(chunks * shards)
    chosen = jnp.sum(
        (slots[:, None] == lane[None, :]).astype(jnp.int32) * (at % deep)[None, :], axis=1
    )
    wanted = lax.dynamic_index_in_dim(new_units, mp_index, 0, False)
    arrive = (place % chunks * shards + iota(shards)[:, None]).reshape(-1)
    found = (wanted[:, None] == iota(total)[None, :]).astype(jnp.int32)
    landed = jnp.sum(found * arrive[None, :], axis=1)
    return order, chosen, landed


def exact_parts(values):
    high = values.astype(jnp.bfloat16)
    rest = values - high.astype(jnp.float32)
    middle = rest.astype(jnp.bfloat16)
    low = (rest - middle.astype(jnp.float32)).astype(jnp.bfloat16)
    return jnp.concatenate([high, middle, low], axis=1)


def exact_pick(pairs):
    out = None
    for onehot, parts in pairs:
        term = jnp.dot(onehot, parts, preferred_element_type=jnp.float32)
        out = term if out is None else out + term
    width = out.shape[1] // 3
    return (out[:, :width] + out[:, width : 2 * width]) + out[:, 2 * width :]


SLOTS = 3
SKEW = 2


def move_kernel(dp, mp, rows, units, room, chunks, *refs):
    order_ref, chosen_ref = refs[:2]
    right_own, right_fwd, left_own, left_fwd, new_own, new_right, new_left = refs[2:9]
    states = refs[9:12]
    out_ref = refs[12]
    (held, from_left, from_right, to_right, to_left, placed, unit_leave) = refs[13:20]
    (load_sem, right_send, right_recv, left_send, left_recv, unit_send, unit_recv, own_sem, tail_send, tail_recv) = refs[
        20:
    ]
    me = lax.axis_index("dp")
    me_mp = lax.axis_index("mp")
    last = dp - 1
    deep = -(-units // chunks)

    def load(u, carry):
        for a in range(3):
            pltpu.make_async_copy(
                states[a].at[:, pl.ds(pl.multiple_of(u * UNIT, UNIT), UNIT)],
                held.at[a, u],
                load_sem.at[a],
            ).start()
        return carry

    lax.fori_loop(0, units, load, 0)
    barrier = pltpu.get_barrier_semaphore()

    for k in (1, last):
        pl.semaphore_signal(
            barrier, inc=1, device_id=(lax.rem(me + k, dp), me_mp), device_id_type=MESH
        )
    for k in range(1, mp):
        pl.semaphore_signal(
            barrier, inc=1, device_id=(me, lax.rem(me_mp + k, mp)), device_id_type=MESH
        )
    pl.semaphore_wait(barrier, mp + 1)

    def right_copy(i):
        return pltpu.make_async_remote_copy(
            src_ref=to_right.at[lax.rem(i, SLOTS)],
            dst_ref=from_left.at[i],
            send_sem=right_send.at[lax.rem(i, SLOTS)],
            recv_sem=right_recv.at[i],
            device_id=(me + 1, me_mp),
            device_id_type=MESH,
        )

    def left_copy(i):
        return pltpu.make_async_remote_copy(
            src_ref=to_left.at[lax.rem(i, SLOTS)],
            dst_ref=from_right.at[i],
            send_sem=left_send.at[lax.rem(i, SLOTS)],
            recv_sem=left_recv.at[i],
            device_id=(me - 1, me_mp),
            device_id_type=MESH,
        )

    starts = [j * (units // chunks) + min(j, units % chunks) for j in range(chunks + 1)]
    final = starts[chunks - 1]
    tail = units - final

    def piece(i, q):
        p = jnp.maximum(i - final, 0) * 3 + q
        early = i < final
        return jnp.where(early, q, p // tail), jnp.where(early, i, final + lax.rem(p, tail))

    def own_parts(i):
        pieces = []
        for q in range(3):
            a, at = piece(i, q)
            pieces.append(held[a, order_ref[at]])
        return exact_parts(jnp.concatenate(pieces, axis=1))

    def stream_parts(ref, i, there):
        values = jnp.concatenate([ref[i, a] for a in range(3)], axis=1)
        return exact_parts(jnp.where(there, values, 0.0))

    def send_step(i, sends, receives, copy, stage, arriving, own, forward):
        @pl.when(sends & (i >= 0) & (i < units))
        def _():
            @pl.when(receives)
            def _():
                copy(i).wait_recv()

            @pl.when(i >= SLOTS)
            def _():
                copy(i - SLOTS).wait_send()

            picked = exact_pick(
                [(own[...], own_parts(i)), (forward[...], stream_parts(arriving, i, receives))]
            )
            for a in range(3):
                stage[lax.rem(i, SLOTS), a] = picked[:, a * UNIT : (a + 1) * UNIT]
            copy(i).start()

    def sends(t):
        send_step(
            t - SKEW * me, me < last, me > 0, right_copy, to_right, from_left, right_own, right_fwd
        )
        send_step(
            t - SKEW * (last - me), me > 0, me < last, left_copy, to_left, from_right, left_own, left_fwd
        )

    def place(i):
        @pl.when(me == last)
        def _():
            right_copy(i).wait_recv()

        @pl.when(me == 0)
        def _():
            left_copy(i).wait_recv()

        picked = exact_pick(
            [
                (new_own[...], own_parts(i)),
                (new_right[...], stream_parts(from_left, i, me > 0)),
                (new_left[...], stream_parts(from_right, i, me < last)),
            ]
        )
        for q in range(3):
            a, at = piece(i, q)
            placed[lax.rem(at, deep), a] = picked[:, q * UNIT : (q + 1) * UNIT]

    def unit_copy(j, k):
        return pltpu.make_async_remote_copy(
            src_ref=unit_leave.at[j % 2, k],
            dst_ref=out_ref.at[j * mp + me_mp],
            send_sem=unit_send.at[j % 2, k],
            recv_sem=unit_recv.at[j, k],
            device_id=(me, lax.rem(me_mp + k, mp)),
            device_id_type=MESH,
        )

    def own_copy(j):
        return pltpu.make_async_copy(
            unit_leave.at[j % 2, 0], out_ref.at[j * mp + me_mp], own_sem.at[j % 2]
        )

    def tail_copy(a, k):
        j = chunks - 1
        return pltpu.make_async_remote_copy(
            src_ref=unit_leave.at[j % 2, k, a],
            dst_ref=out_ref.at[j * mp + me_mp, a],
            send_sem=tail_send.at[a, k],
            recv_sem=tail_recv.at[a, k],
            device_id=(me, lax.rem(me_mp + k, mp)),
            device_id_type=MESH,
        )

    def tail_own(a):
        j = chunks - 1
        return pltpu.make_async_copy(
            unit_leave.at[j % 2, 0, a], out_ref.at[j * mp + me_mp, a], tail_send.at[a, 0]
        )

    def gather(j, arrays):
        def one(k, carry):
            w = chosen_ref[j * mp + lax.rem(me_mp + k, mp)]
            for a in arrays:
                unit_leave[j % 2, k, a] = placed[w, a]
            return carry

        lax.fori_loop(0, mp, one, 0)

    def wait_unit_send(j):
        for k in range(1, mp):
            unit_copy(j, k).wait_send()
        own_copy(j).wait()

    def emit(j):
        if j >= 2:
            wait_unit_send(j - 2)
        gather(j, range(3))
        own_copy(j).start()

    def emit_tail(a):
        if a == 0 and chunks >= 3:
            wait_unit_send(chunks - 3)
        gather(chunks - 1, [a])
        for k in range(1, mp):
            tail_copy(a, k).start()
        tail_own(a).start()

    for a in range(3):
        pltpu.make_async_copy(held.at[a], held.at[a], load_sem.at[a]).wait()

    lead = SKEW * last

    burst = -(-(mp - 1) // max(min(3, units // chunks, tail), 1))

    def step(t, carry):
        sends(t)
        i = t - lead

        @pl.when(i >= 0)
        def _():
            place(i)

        for j in range(chunks - 1):

            @pl.when(i == starts[j + 1] - 1)
            def _():
                emit(j)

            for n, k in enumerate(range(1, mp, burst)):

                @pl.when(i == starts[j + 1] - 1 + n)
                def _():
                    for peer in range(k, min(k + burst, mp)):
                        unit_copy(j, peer).start()

        for a in range(3):

            @pl.when(i == final - 1 + -(-tail * (a + 1) // 3))
            def _():
                emit_tail(a)

        return carry

    lax.fori_loop(0, lead + units, step, 0)

    for i in range(max(units - SLOTS, 0), units):

        @pl.when(me < last)
        def _():
            right_copy(i).wait_send()

        @pl.when(me > 0)
        def _():
            left_copy(i).wait_send()

    if chunks >= 2:
        wait_unit_send(chunks - 2)
    for a in range(3):
        for k in range(1, mp):
            tail_copy(a, k).wait_send()
        tail_own(a).wait()
    for j in range(chunks - 1):
        for k in range(1, mp):
            unit_copy(j, k).wait_recv()
    for a in range(3):
        for k in range(1, mp):
            tail_copy(a, k).wait_recv()


def move(order, chosen, matrices, states, dp, mp, rows, units, room, chunks, collective_id):
    deep = -(-units // chunks)
    vmem = pl.BlockSpec(memory_space=pltpu.VMEM)
    smem = pl.BlockSpec(memory_space=pltpu.SMEM)
    f32 = jnp.float32
    dma = pltpu.SemaphoreType.DMA
    return pl.pallas_call(
        functools.partial(move_kernel, dp, mp, rows, units, room, chunks),
        out_shape=jax.ShapeDtypeStruct((chunks * mp, 3, rows, UNIT), f32),
        in_specs=[smem, smem] + [vmem] * 7 + [pl.BlockSpec(memory_space=pl.ANY)] * 3,
        out_specs=pl.BlockSpec(memory_space=pl.ANY),
        scratch_shapes=[
            pltpu.VMEM((3, units, rows, UNIT), f32),
            pltpu.VMEM((units, 3, room, UNIT), f32),
            pltpu.VMEM((units, 3, room, UNIT), f32),
            pltpu.VMEM((SLOTS, 3, room, UNIT), f32),
            pltpu.VMEM((SLOTS, 3, room, UNIT), f32),
            pltpu.VMEM((deep, 3, rows, UNIT), f32),
            pltpu.VMEM((2, mp, 3, rows, UNIT), f32),
            dma((3,)),
            dma((SLOTS,)),
            dma((units,)),
            dma((SLOTS,)),
            dma((units,)),
            dma((2, mp)),
            dma((chunks, mp)),
            dma((2,)),
            dma((3, mp)),
            dma((3, mp)),
        ],
        compiler_params=pltpu.CompilerParams(
            collective_id=collective_id, has_side_effects=True, vmem_limit_bytes=60 * 2**20
        ),
    )(order, chosen, *matrices, *states)


def move_any(order, chosen, target, old_rows, new_rows, states, me, mp, units, chunks):
    dp, per = old_rows.shape
    room = room_for(per, dp)
    target = target.reshape(dp, per)
    earlier = (iota(per)[:, None] > iota(per)[None, :])[None]
    rank = jnp.sum(((target[:, :, None] == target[:, None, :]) & earlier).astype(jnp.int32), axis=2)
    spot = lax.dynamic_index_in_dim(target * room + rank, me, 0, False)
    hit = (iota(dp * room)[:, None] == spot[None, :]).astype(jnp.int32)
    pack = jnp.sum(hit * iota(per)[None, :], axis=1)
    anchor = (iota(dp * per) // per) * room + rank.reshape(-1)
    wanted = lax.dynamic_index_in_dim(new_rows, me, 0, False)
    found = (wanted[:, None] == old_rows.reshape(-1)[None, :]).astype(jnp.int32)
    take = jnp.sum(found * anchor[None, :], axis=1)
    begin = jnp.array(
        [j * (units // chunks) + min(j, units % chunks) for j in range(chunks)], jnp.int32
    )
    deep = -(-units // chunks)
    first = jnp.repeat(begin, mp)
    slots = jnp.take(order, first + (chosen - first + deep * chunks) % deep, mode="clip")
    moved = []
    for state in states:
        packed = jnp.take(state, pack, axis=0)
        arrived = lax.all_to_all(packed, "dp", split_axis=0, concat_axis=0, tiled=True)
        rowed = jnp.take(arrived, take, axis=0).reshape(per, units, UNIT)
        leave = jnp.take(rowed, slots, axis=1).reshape(per, chunks, mp, UNIT)
        came = lax.all_to_all(leave, "mp", split_axis=2, concat_axis=2, tiled=True)
        moved.append(came.reshape(per, chunks * mp, UNIT).transpose(1, 0, 2))
    return jnp.stack(moved, axis=1)


def adam_kernel(group, landed_ref, fix_ref, *refs):
    moved = refs[:group]
    gradient_ref = refs[group]
    weight_out, first_out, second_out, update_out = refs[group + 1 :]
    first_fix = fix_ref[0]
    second_fix = fix_ref[1]
    for g in range(group):
        at = slice(g * UNIT, (g + 1) * UNIT)
        weight, first, second = moved[g][0, 0], moved[g][0, 1], moved[g][0, 2]
        gradient = gradient_ref[:, at]
        new_first = beta_one * first + (1.0 - beta_one) * gradient
        new_second = beta_two * second + (1.0 - beta_two) * gradient * gradient
        update = (
            new_first * first_fix / (jnp.sqrt(new_second * second_fix) + epsilon)
            + decay_rate * weight
        )
        weight_out[:, at] = weight - learn_rate * update
        first_out[:, at] = new_first
        second_out[:, at] = new_second
        update_out[:, at] = update


def adam(landed, fixes, moved, gradient):
    rows, columns = gradient.shape
    units = columns // UNIT
    group = next(g for g in (3, 2, 1) if units % g == 0)
    wide = pl.BlockSpec((rows, group * UNIT), lambda i, landed: (0, i))
    picks = [
        pl.BlockSpec((1, 3, rows, UNIT), lambda i, landed, g=g: (landed[i * group + g], 0, 0, 0))
        for g in range(group)
    ]
    return pl.pallas_call(
        functools.partial(adam_kernel, group),
        out_shape=[jax.ShapeDtypeStruct((rows, columns), jnp.float32)] * 4,
        grid_spec=pltpu.PrefetchScalarGridSpec(
            num_scalar_prefetch=1,
            grid=(units // group,),
            in_specs=[pl.BlockSpec(memory_space=pltpu.SMEM)] + picks + [wide],
            out_specs=[wide] * 4,
        ),
        compiler_params=pltpu.CompilerParams(vmem_limit_bytes=60 * 2**20),
    )(landed, fixes, *([moved] * group), gradient)


def body(old_weight, old_first, old_second, gradient, old_rows, new_rows, new_units, step):
    dp = lax.axis_size("dp")
    mp = lax.axis_size("mp")
    rows = old_weight.shape[0]
    units = new_units.shape[1]
    chunks = room_for(units, mp)
    me = lax.axis_index("dp")
    order, chosen, landed = unit_plan(new_units, lax.axis_index("mp"), chunks)
    target = row_targets(old_rows, new_rows)
    local, place, taken = row_streams(target, old_rows, new_rows, me)
    states = (old_weight, old_first, old_second)
    even = rows * dp // 4
    rooms = sorted({-(-even * part // 64) * 8 for part in (7, 8, 9, 10)})

    count = step[0].astype(jnp.float32)
    fixes = jnp.stack(
        [
            1.0 / (1.0 - jnp.power(jnp.float32(beta_one), count)),
            1.0 / (1.0 - jnp.power(jnp.float32(beta_two), count)),
        ]
    )

    def moved_in(room, collective_id):
        matrices = row_matrices(local, place, taken, me, rows, room)
        moved = move(
            order, chosen, matrices, states, dp, mp, rows, units, room, chunks, collective_id
        )
        return adam(landed, fixes, moved, gradient)

    def moved_any():
        moved = move_any(
            order, chosen, target, old_rows, new_rows, states, me, mp, units, chunks
        )
        return adam(landed, fixes, moved, gradient)

    need = row_needs(target, dp, rows)
    level = sum((need > room).astype(jnp.int32) for room in rooms)
    branches = [functools.partial(moved_in, room, n) for n, room in enumerate(rooms)]
    outs = lax.switch(level, branches + [moved_any])
    return tuple(outs)


def solution(mesh):
    return jax.shard_map(
        body,
        mesh=mesh,
        in_specs=(P("dp", "mp"), P("dp", "mp"), P("dp", "mp"), P("dp", "mp"), P(), P(), P(), P()),
        out_specs=(P("dp", "mp"), P("dp", "mp"), P("dp", "mp"), P("dp", "mp")),
        check_vma=False,
    )
```
